32 devices in a mesh: fsdp: 16 (over z, y, core), seq: 2 (over x).
Axes of the slice: x: 2, y: 2, z: 4, core: 2. Of those that a mesh axis runs over, the one named last changes fastest.
Arguments:
- hidden_in: bfloat16 [8192, 1536], P(('fsdp', 'seq')), may hold values from -6 to 6
- grad_out: bfloat16 [8192, 1536], P(('fsdp', 'seq')), may hold values from -7.5 to 7.5
- routes: int32 [8192, 8], P(('fsdp', 'seq')), may hold values from 0 to 39, all different within a row; in each aligned block of 256 rows (0 to 255, 256 to 511, ...) at most 76 rows name the same one
- gate_weights: bfloat16 [8192, 8], P(('fsdp', 'seq')), may hold values from 0.059814453 to 0.25
- doc_start: int32 [8192], P('fsdp'), may hold values from 0 to 8191, as said below
- qkv_weight: float32 [1536, 2560], P(('fsdp', 'seq')), may hold values from -1.14819832 to 1.14819832
- qkv_first: float32 [1536, 2560], P(('fsdp', 'seq')), may hold values from -24 to 24
- qkv_second: float32 [1536, 2560], P(('fsdp', 'seq')), may hold values from 0.65536 to 10.48576
- out_weight: float32 [1536, 1536], P(None, ('fsdp', 'seq')), may hold values from -3.75 to 3.75
- out_first: float32 [1536, 1536], P(None, ('fsdp', 'seq')), may hold values from -3 to 3
- out_second: float32 [1536, 1536], P(None, ('fsdp', 'seq')), may hold values from 0.01024 to 0.16384
- norm_gains: float32 [2, 1536], P(None, ('fsdp', 'seq')), may hold values from 0.35 to 1.95
- gains_first: float32 [2, 1536], P(None, ('fsdp', 'seq')), may hold values from -96 to 96
- gains_second: float32 [2, 1536], P(None, ('fsdp', 'seq')), may hold values from 9.0112 to 144.1792
- gate_weight: float32 [40, 1536, 512], P('seq', 'fsdp'), may hold values from -0.19136639 to 0.19136639
- gate_first: float32 [40, 1536, 512], P('seq', 'fsdp'), may hold values from -14 to 14
- gate_second: float32 [40, 1536, 512], P('seq', 'fsdp'), may hold values from 0.20475 to 3.276
- up_weight: float32 [40, 1536, 512], P('seq', 'fsdp'), may hold values from -0.19136639 to 0.19136639
- up_first: float32 [40, 1536, 512], P('seq', 'fsdp'), may hold values from -14 to 14
- up_second: float32 [40, 1536, 512], P('seq', 'fsdp'), may hold values from 0.20475 to 3.276
- down_weight: float32 [40, 512, 1536], P('seq', None, 'fsdp'), may hold values from -7.32 to 7.32
- down_first: float32 [40, 512, 1536], P('seq', None, 'fsdp'), may hold values from -0.625 to 0.625
- down_second: float32 [40, 512, 1536], P('seq', None, 'fsdp'), may hold values from 0.0004914 to 0.0078624
Outputs:
- block_output: bfloat16 [8192, 1536], P(('fsdp', 'seq'))
- input_grad: float32 [8192, 1536], P(('fsdp', 'seq'))
- qkv_master: float32 [1536, 2560], P(('fsdp', 'seq'))
- qkv_momentum: float32 [1536, 2560], P(('fsdp', 'seq'))
- qkv_variance: float32 [1536, 2560], P(('fsdp', 'seq'))
- out_master: float32 [1536, 1536], P(None, ('fsdp', 'seq'))
- out_momentum: float32 [1536, 1536], P(None, ('fsdp', 'seq'))
- out_variance: float32 [1536, 1536], P(None, ('fsdp', 'seq'))
- gains_master: float32 [2, 1536], P(None, ('fsdp', 'seq'))
- gains_momentum: float32 [2, 1536], P(None, ('fsdp', 'seq'))
- gains_variance: float32 [2, 1536], P(None, ('fsdp', 'seq'))
- gate_master: float32 [40, 1536, 512], P('seq', 'fsdp')
- gate_momentum: float32 [40, 1536, 512], P('seq', 'fsdp')
- gate_variance: float32 [40, 1536, 512], P('seq', 'fsdp')
- up_master: float32 [40, 1536, 512], P('seq', 'fsdp')
- up_momentum: float32 [40, 1536, 512], P('seq', 'fsdp')
- up_variance: float32 [40, 1536, 512], P('seq', 'fsdp')
- down_master: float32 [40, 512, 1536], P('seq', None, 'fsdp')
- down_momentum: float32 [40, 512, 1536], P('seq', None, 'fsdp')
- down_variance: float32 [40, 512, 1536], P('seq', None, 'fsdp')
- clip_factors: float32 [24], replicated
- lamb_norms: float32 [2, 7], replicated
The draws below stay inside these ranges and needn't reach their ends.
Inputs may be any that keep to these rules, and one draw needn't show every extreme that they name: doc_start never falls, doc_start[t] <= t, and a document begins at t exactly where doc_start[t] = t; every document has at most 512 tokens and one has exactly 512. `routes`: in the rows of one device no expert is named by more than 76 (token, choice) pairs.
All inputs are finite; a program needn't handle non-finite values.
Results may differ from the reference program's by a relative error of at most 0.023.
The reference program's roundings to bfloat16 on the way count: a program that leaves them out, or rounds other values in their place, can miss the bound.
Values may be sent and summed in bfloat16 or wider, within the bound.
A program may use at most 384 MiB of HBM per device.

```python
import math
import jax
import jax.numpy as jnp
import numpy as np
from jax import lax

D = 1536
NH = 24
KVH = 8
HD = 64
FF = 512
EXPERTS = 40
TOP = 8
TOK_DEV = 256
STEP = 10
QKV = 2560
GROUP = 512
TOKENS = 8192
CAP = 76
QBLOCK = 512
N_SEQ = 2


def rising(count):
    return 0.5 + jnp.arange(count, dtype=jnp.float32) / count


def draw_doc_start(key, part):
    key = jax.random.fold_in(key, 11)
    groups = TOKENS // GROUP
    half_width = TOK_DEV // 2
    begin_key, finish_key, cut_key = jax.random.split(key, 3)
    begin = jax.random.randint(begin_key, (groups,), half_width, TOK_DEV, dtype=jnp.int32).at[0].set(half_width)
    finish = jax.random.randint(finish_key, (groups,), 1, half_width + 1, dtype=jnp.int32).at[0].set(half_width)
    leading = jnp.zeros((1,), jnp.int32)
    earlier = jnp.concatenate([leading, finish[:-1]])
    begin_before = jnp.concatenate([leading, begin[:-1]])
    cut_point = earlier + jax.random.randint(cut_key, (groups,), 0, TOK_DEV, dtype=jnp.int32) % (begin - earlier + 1)
    position = jnp.arange(TOKENS, dtype=jnp.int32)
    group_of = position // GROUP
    local = position % GROUP
    base = group_of * GROUP
    return jnp.where(local >= begin[group_of], base + begin[group_of], jnp.where(local < earlier[group_of], base - GROUP + begin_before[group_of], jnp.where(local < cut_point[group_of], base + earlier[group_of], base + cut_point[group_of])))


def draw_grad_out(key, part):
    key = jax.random.fold_in(key, 2)
    sample = jnp.clip(jax.random.normal(key, (TOKENS, D), jnp.float32), -5.0, 5.0)
    return (sample * rising(D)[None, :]).astype(jnp.bfloat16)


def draw_qkv_weight(key, part):
    key = jax.random.fold_in(key, 3)
    noise_key, order_key = jax.random.split(key)
    sample = jnp.clip(jax.random.normal(noise_key, (D, QKV), jnp.float32), -5.0, 5.0)
    head_order = jax.random.permutation(order_key, NH).astype(jnp.float32)
    head_scale = 0.8 * 3.0 ** (head_order / (NH - 1))
    per_kv = NH // KVH
    head_columns = jnp.repeat(head_scale.reshape(KVH, per_kv), HD, axis=1)
    columns = jnp.concatenate([head_columns, jnp.ones((KVH, 2 * HD), jnp.float32)], axis=1).reshape(QKV)
    return sample * (2.5 / D ** 0.5) * rising(D)[:, None] * columns[None, :]


def draw_out_weight(key, part):
    key = jax.random.fold_in(key, 4)
    sample = jnp.clip(jax.random.normal(key, (NH * HD, D), jnp.float32), -5.0, 5.0)
    return sample * 0.5 * rising(D)[None, :]


def draw_norm_gains(key, part):
    key = jax.random.fold_in(key, 5)
    factor = jax.random.uniform(key, (2, D), jnp.float32, 0.85, 1.15)
    return factor * rising(D)[None, :]


def draw_gate_weight(key, part):
    key = jax.random.fold_in(key, 6)
    sample = jnp.clip(jax.random.normal(key, (EXPERTS, D, FF), jnp.float32), -5.0, 5.0)
    return sample * (1.0 / D ** 0.5) * rising(D)[None, :, None]


def draw_up_weight(key, part):
    key = jax.random.fold_in(key, 7)
    sample = jnp.clip(jax.random.normal(key, (EXPERTS, D, FF), jnp.float32), -5.0, 5.0)
    return sample * (1.0 / D ** 0.5) * rising(D)[None, :, None]


def draw_down_weight(key, part):
    key = jax.random.fold_in(key, 8)
    sample = jnp.clip(jax.random.normal(key, (EXPERTS, FF, D), jnp.float32), -5.0, 5.0)
    return sample * 0.65 * rising(D)[None, None, :] * rising(EXPERTS)[:, None, None]


def levels(rng, shape, shards, smallest, top_value):
    factor_of, own = 1.0, jax.random.fold_in(rng, 6)
    for dim, blocks in shards:
        draws = jnp.exp(jax.random.uniform(jax.random.fold_in(own, dim), (blocks,), jnp.float32, smallest / len(shards), top_value / len(shards)))
        factor_of = factor_of * jnp.repeat(draws, shape[dim] // blocks).reshape([-1 if axis == dim else 1 for axis in range(len(shape))])
    return factor_of


def routed_block(own_key, own, number, rows, count, top, bound, lean):
    sequence = jax.random.permutation(own_key, count)
    heavy_load, common = shares(count, rows * top, bound, lean, True), shares(count, rows * top, bound, lean, False)
    places = jnp.arange(count)

    def named(sizes, offset_by):
        used = int((sizes > 0).sum())
        fixed = max(1, used // 4)
        shifted = fixed + (places - fixed + offset_by * (used - fixed)) % max(1, count - fixed)
        return jnp.zeros((count,), jnp.int32).at[sequence[jnp.where(places < fixed, places, shifted)]].set(jnp.asarray(sizes, jnp.int32))

    sizes = jnp.where(number % 4 == 0, named(heavy_load, number // 4), named(common, number - number // 4 - 1))
    mixed = jax.random.permutation(jax.random.fold_in(own, 3), count)
    giver, sink = mixed[0:count // 2 * 2:2], mixed[1:count // 2 * 2:2]
    room = jnp.minimum(sizes[giver] - 1, bound - sizes[sink]) // 2
    room = jnp.where((giver == sequence[0]) | (sink == sequence[0]) | (sizes[sink] == 0), 0, jnp.maximum(room, 0))
    shifted = jax.random.randint(jax.random.fold_in(own, 4), (count // 2,), 0, 1 << 20) % (room + 1)
    sizes = sizes.at[giver].add(-shifted).at[sink].add(shifted)
    members = jnp.searchsorted(jnp.cumsum(sizes), jnp.arange(rows * top), side="right").astype(jnp.int32)
    listing = members.reshape(top, rows).T
    listing = listing[jax.random.permutation(jax.random.fold_in(own, 1), rows)]
    offset_by = jax.random.randint(jax.random.fold_in(own, 2), (rows, 1), 0, top)
    return jnp.take_along_axis(listing, (jnp.arange(top)[None, :] + offset_by) % top, axis=1)


def shares(number_of, total, bound, lean, full):
    loads = [(1 << 20) // math.isqrt(grade ** lean) + 1 for grade in range(1, number_of + 1)]
    largest = bound if full else min(bound, max(-(-total // number_of), total * loads[0] // sum(loads)))
    least = 1 if total - largest >= number_of - 1 else 0
    given, surplus = [largest] + [least] * (number_of - 1), total - largest - least * (number_of - 1)
    while surplus > 0:
        movable = [i for i in range(1, number_of) if given[i] < largest] or [i for i in range(1, number_of) if given[i] < bound]
        whole, remaining = sum([loads[i] for i in movable]), surplus
        for i in movable:
            more = min(bound - given[i], max(1, remaining * loads[i] // whole), surplus)
            given[i] = given[i] + more
            surplus = surplus - more
    return np.array(given)


def noise(own_key, dims, scale, most, shards=(), kind=jnp.bfloat16):
    drawn = scale * jax.random.normal(own_key, dims, jnp.float32)
    if shards:
        drawn = drawn * levels(own_key, dims, shards, -0.22, 0.18)
    return jnp.clip(drawn, -most, most).astype(kind)


def setup_inputs(seed: int = 0) -> dict:
    splits = jax.random.split(jax.random.key(seed), 24)
    hidden_in = noise(splits[0], (TOKENS, D), 1.0, 6.0, ((0, 32),))
    grad_out = draw_grad_out(jax.random.fold_in(splits[23], 71), 0)
    routes_keys = jax.random.split(jax.random.fold_in(splits[2], 1), TOKENS // TOK_DEV)
    routes_turns = jax.random.permutation(jax.random.fold_in(splits[2], 3), TOKENS // TOK_DEV)
    routes = jax.vmap(lambda own, number: routed_block(jax.random.fold_in(splits[2], 2), own, number, TOK_DEV, EXPERTS, TOP, CAP, 1))(routes_keys, routes_turns).reshape((TOKENS, TOP))
    gate_weights = jnp.clip(jnp.exp(math.log(0.25) - 1.4302136 * jax.random.uniform(splits[3], (TOKENS, TOP), jnp.float32) ** levels(splits[3], (TOKENS, TOP), ((0, 32),), -0.2, 0.2)), 0.059814453, 0.25).astype(jnp.bfloat16)
    doc_start = draw_doc_start(jax.random.fold_in(splits[23], 71), 0)
    qkv_weight = draw_qkv_weight(jax.random.fold_in(splits[23], 71), 0)
    qkv_first = noise(splits[6], (D, QKV), (0.044 * TOKENS ** 0.5), 24.0, ((0, 32),), jnp.float32)
    qkv_second = jnp.clip(jnp.exp(math.log(10.48576) - 2.7725887 * jax.random.uniform(splits[7], (D, QKV), jnp.float32) ** levels(splits[7], (D, QKV), ((0, 32),), -0.2, 0.2)), 0.65536, 10.48576)
    out_weight = draw_out_weight(jax.random.fold_in(splits[23], 71), 0)
    out_first = noise(splits[9], (NH * HD, D), (0.0056 * TOKENS ** 0.5), 3.0, ((1, 32),), jnp.float32)
    out_second = jnp.clip(jnp.exp(math.log(0.16384) - 2.7725887 * jax.random.uniform(splits[10], (NH * HD, D), jnp.float32) ** levels(splits[10], (NH * HD, D), ((1, 32),), -0.2, 0.2)), 0.01024, 0.16384)
    norm_gains = draw_norm_gains(jax.random.fold_in(splits[23], 71), 0)
    gains_first = noise(splits[12], (2, D), (0.165 * TOKENS ** 0.5), 96.0, ((1, 32),), jnp.float32)
    gains_second = jnp.clip(jnp.exp(math.log(144.1792) - 2.7725887 * jax.random.uniform(splits[13], (2, D), jnp.float32) ** levels(splits[13], (2, D), ((1, 32),), -0.2, 0.2)), 9.0112, 144.1792)
    gate_weight = draw_gate_weight(jax.random.fold_in(splits[23], 71), 0)
    gate_first = noise(splits[15], (EXPERTS, D, FF), (0.055 * (TOKENS * TOP // EXPERTS) ** 0.5), 14.0, ((0, 2), (1, 16)), jnp.float32)
    gate_second = jnp.clip(jnp.exp(math.log(3.276) - 2.7725887 * jax.random.uniform(splits[16], (EXPERTS, D, FF), jnp.float32) ** levels(splits[16], (EXPERTS, D, FF), ((0, 2), (1, 16)), -0.2, 0.2)), 0.20475, 3.276)
    up_weight = draw_up_weight(jax.random.fold_in(splits[23], 71), 0)
    up_first = noise(splits[18], (EXPERTS, D, FF), (0.055 * (TOKENS * TOP // EXPERTS) ** 0.5), 14.0, ((0, 2), (1, 16)), jnp.float32)
    up_second = jnp.clip(jnp.exp(math.log(3.276) - 2.7725887 * jax.random.uniform(splits[19], (EXPERTS, D, FF), jnp.float32) ** levels(splits[19], (EXPERTS, D, FF), ((0, 2), (1, 16)), -0.2, 0.2)), 0.20475, 3.276)
    down_weight = draw_down_weight(jax.random.fold_in(splits[23], 71), 0)
    down_first = noise(splits[21], (EXPERTS, FF, D), (0.0027 * (TOKENS * TOP // EXPERTS) ** 0.5), 0.625, ((0, 2), (2, 16)), jnp.float32)
    down_second = jnp.clip(jnp.exp(math.log(0.0078624) - 2.7725887 * jax.random.uniform(splits[22], (EXPERTS, FF, D), jnp.float32) ** levels(splits[22], (EXPERTS, FF, D), ((0, 2), (2, 16)), -0.2, 0.2)), 0.0004914, 0.0078624)
    return dict(hidden_in=hidden_in, grad_out=grad_out, routes=routes, gate_weights=gate_weights, doc_start=doc_start, qkv_weight=qkv_weight, qkv_first=qkv_first, qkv_second=qkv_second, out_weight=out_weight, out_first=out_first, out_second=out_second, norm_gains=norm_gains, gains_first=gains_first, gains_second=gains_second, gate_weight=gate_weight, gate_first=gate_first, gate_second=gate_second, up_weight=up_weight, up_first=up_first, up_second=up_second, down_weight=down_weight, down_first=down_first, down_second=down_second)


RESIDUAL_SCALE = 0.22
SCORE_SCALE = 0.015625
NORM_EPS = 1e-06
ROPE_BASE = 10000.0
CLIP_BASE = 4.5
BETA_ONE = 0.9
BETA_TWO = 0.999
ADAM_EPS = 1e-06
WEIGHT_DECAY = 0.01
LEARN_RATE = 0.3
MASK_FILL = -1e+30
HIGHEST = lax.Precision.HIGHEST

@jax.custom_vjp
def low(v):
    return lax.optimization_barrier(v.astype(jnp.bfloat16)).astype(jnp.float32)

@jax.custom_vjp
def low_back(v):
    return v

def low_keep(v):
    return (low(v), None)

def low_pass(kept, grad):
    return (grad,)

def back_keep(v):
    return (v, None)

def back_low(kept, grad):
    return (low(grad),)
low.defvjp(low_keep, low_pass)
low_back.defvjp(back_keep, back_low)

def rms_norm(values, gain):
    return values * lax.rsqrt(lax.optimization_barrier(jnp.mean(values * values, axis=-1, keepdims=True)) + NORM_EPS) * gain

def rope_tables(positions, head_width):
    half_width = head_width // 2
    frequency = ROPE_BASE ** (-(jnp.arange(half_width, dtype=jnp.float32) * (2.0 / head_width)))
    angles = positions.astype(jnp.float32)[:, None] * frequency[None, :]
    return (jnp.cos(angles), jnp.sin(angles))

def rotate(values, cos_table, sin_table):
    half_width = values.shape[-1] // 2
    view_shape = (cos_table.shape[0],) + (1,) * (values.ndim - 2) + (half_width,)
    cos_view = cos_table.reshape(view_shape)
    sin_view = sin_table.reshape(view_shape)
    first_half = values[..., :half_width]
    second_half = values[..., half_width:]
    return jnp.concatenate([first_half * cos_view - second_half * sin_view, second_half * cos_view + first_half * sin_view], axis=-1)

def slot_table(routed, expert_count, capacity):
    flat_routes = routed.reshape(-1).astype(jnp.int32)
    row_count = flat_routes.shape[0]
    onehot = (flat_routes[:, None] == jnp.arange(expert_count, dtype=jnp.int32)[None, :]).astype(jnp.int32)
    slot_rank = lax.optimization_barrier(jnp.sum((jnp.cumsum(onehot, axis=0) - 1) * onehot, axis=1)).astype(jnp.int32)
    target = (flat_routes * capacity + slot_rank).astype(jnp.int32)
    sources = jnp.full((expert_count * capacity,), row_count, jnp.int32).at[target].set(jnp.arange(row_count, dtype=jnp.int32))
    return (sources, target)

def column_scale(factor):
    per_kv = NH // KVH
    head_part = jnp.repeat(factor.reshape(KVH, per_kv), HD, axis=1)
    return jnp.concatenate([head_part, jnp.ones((KVH, 2 * HD), factor.dtype)], axis=1).reshape(-1)

def adam_direction(weight_now, gradient, mean_old, square_old):
    momentum = BETA_ONE * mean_old + (1.0 - BETA_ONE) * gradient
    variance = BETA_TWO * square_old + (1.0 - BETA_TWO) * gradient * gradient
    direction = momentum / (1.0 - BETA_ONE ** STEP) / (jnp.sqrt(variance / (1.0 - BETA_TWO ** STEP)) + ADAM_EPS) + WEIGHT_DECAY * weight_now
    return (momentum, variance, direction)

def attend_group(group_args):
    queries, keys_all, values_all, starts, offset = group_args
    per_kv = NH // KVH
    blocks = GROUP // QBLOCK
    key_pos = offset - GROUP + jnp.arange(2 * GROUP, dtype=jnp.int32)
    query_pos = (offset + jnp.arange(GROUP, dtype=jnp.int32)).reshape(blocks, QBLOCK)

    def one_block(block_args):
        block_q, block_start, block_pos = block_args
        allowed = (key_pos[None, :] >= block_start[:, None]) & (key_pos[None, :] <= block_pos[:, None])
        scores = low_back(jnp.einsum('qjid,kjd->jiqk', block_q, keys_all, precision=HIGHEST) * SCORE_SCALE)
        masked = jnp.where(allowed, scores, MASK_FILL)
        row_peak = lax.optimization_barrier(jnp.max(masked, axis=-1, keepdims=True))
        exponent = jnp.where(allowed, jnp.exp(masked - row_peak), 0.0)
        attn_probs = low(exponent / lax.optimization_barrier(jnp.sum(exponent, axis=-1, keepdims=True)))
        attn_mixed = jnp.einsum('jiqk,kjd->qjid', attn_probs, values_all, precision=HIGHEST)
        return (attn_mixed, lax.optimization_barrier(jnp.max(row_peak, axis=(2, 3))))
    block_queries = queries.reshape(blocks, QBLOCK, KVH, per_kv, HD)
    attn_mixed, head_peaks = lax.map(jax.checkpoint(one_block), (block_queries, starts.reshape(blocks, QBLOCK), query_pos))
    return (attn_mixed.reshape(GROUP, NH * HD), lax.optimization_barrier(jnp.max(head_peaks, axis=0)))

def experts_group(rows_in, route_group, gate_group, gate_low, up_low, down_low):
    sources, target = jax.vmap(lambda routed: slot_table(routed, EXPERTS, CAP))(route_group)
    row_count = TOK_DEV * TOP
    token_of = jnp.where(sources < row_count, sources // TOP, TOK_DEV)
    padded = jnp.concatenate([rows_in, jnp.zeros((N_SEQ, 1, D), jnp.float32)], axis=1)
    routed_rows = jax.vmap(lambda lookup, where_from: lookup[where_from])(padded, token_of)
    routed_rows = low_back(routed_rows).reshape(N_SEQ, EXPERTS, CAP, D)
    gate_pre = low_back(jnp.einsum('secd,edf->secf', routed_rows, gate_low, precision=HIGHEST))
    up_pre = low_back(jnp.einsum('secd,edf->secf', routed_rows, up_low, precision=HIGHEST))
    hidden_act = low(jax.nn.silu(gate_pre) * up_pre)
    expert_out = low_back(low(jnp.einsum('secf,efd->secd', hidden_act, down_low, precision=HIGHEST)))
    flat_out = expert_out.reshape(N_SEQ, EXPERTS * CAP, D)
    picked = jax.vmap(lambda lookup, where_from: lookup[where_from])(flat_out, target).reshape(N_SEQ, TOK_DEV, TOP, D)
    return lax.optimization_barrier(jnp.sum(gate_group[..., None] * picked, axis=2))

def reference(hidden_in, grad_out, routes, gate_weights, doc_start, qkv_weight, qkv_first, qkv_second, out_weight, out_first, out_second, norm_gains, gains_first, gains_second, gate_weight, gate_first, gate_second, up_weight, up_first, up_second, down_weight, down_first, down_second):
    per_kv = NH // KVH
    group_width = (per_kv + 2) * HD
    groups = TOKENS // GROUP
    starts_all = doc_start.astype(jnp.int32)
    positions = jnp.arange(TOKENS, dtype=jnp.int32) - starts_all
    cos_table, sin_table = rope_tables(positions, HD)
    starts_grouped = starts_all.reshape(groups, GROUP)
    offsets = jnp.arange(groups, dtype=jnp.int32) * GROUP
    routes_grouped = routes.astype(jnp.int32).reshape(groups, N_SEQ, TOK_DEV, TOP)
    gates_grouped = gate_weights.astype(jnp.float32).reshape(groups, N_SEQ, TOK_DEV, TOP)

    def forward(hidden, w_qkv, w_out, gains, w_gate, w_up, w_down):
        qkv_low = low(w_qkv)
        out_low = low(w_out)
        gain_low = low(gains)
        gate_low = low(w_gate)
        up_low = low(w_up)
        down_low = low(w_down)
        normed_one = low(rms_norm(hidden, gain_low[0]))
        projected = low_back(jnp.dot(normed_one, qkv_low, precision=HIGHEST)).reshape(TOKENS, KVH, group_width)
        turned = rotate(projected[:, :, :(per_kv + 1) * HD].reshape(TOKENS, KVH, per_kv + 1, HD), cos_table, sin_table)
        queries = low(turned[:, :, :per_kv]).reshape(groups, GROUP, KVH, per_kv, HD)
        keys_own = low(turned[:, :, per_kv]).reshape(groups, GROUP, KVH, HD)
        values_own = low(projected[:, :, (per_kv + 1) * HD:]).reshape(groups, GROUP, KVH, HD)
        empty_group = jnp.zeros((1, GROUP, KVH, HD), jnp.float32)
        keys_wide = jnp.concatenate([jnp.concatenate([empty_group, keys_own[:-1]], axis=0), keys_own], axis=1)
        values_wide = jnp.concatenate([jnp.concatenate([empty_group, values_own[:-1]], axis=0), values_own], axis=1)
        attn_mixed, head_peaks = lax.map(jax.checkpoint(attend_group), (queries, keys_wide, values_wide, starts_grouped, offsets))
        attn_mixed = low_back(low(attn_mixed.reshape(TOKENS, NH * HD)))
        after_attn = hidden + RESIDUAL_SCALE * low_back(jnp.dot(attn_mixed, out_low, precision=HIGHEST))
        normed_two = low(rms_norm(after_attn, gain_low[1]))

        def expert_block(block_args):
            return experts_group(block_args[0], block_args[1], block_args[2], gate_low, up_low, down_low)
        mixture = lax.map(jax.checkpoint(expert_block), (normed_two.reshape(groups, N_SEQ, TOK_DEV, D), routes_grouped, gates_grouped))
        block_out = after_attn + RESIDUAL_SCALE * mixture.reshape(TOKENS, D)
        return (block_out, lax.optimization_barrier(jnp.max(head_peaks, axis=0)).reshape(NH))
    block_out, pullback, peak_heads = jax.vjp(forward, hidden_in.astype(jnp.float32), qkv_weight, out_weight, norm_gains, gate_weight, up_weight, down_weight, has_aux=True)
    gradients = pullback(grad_out.astype(jnp.float32))
    weight_list = [qkv_weight, out_weight, norm_gains[0], norm_gains[1], gate_weight, up_weight, down_weight]
    grad_list = [gradients[1], gradients[2], gradients[3][0], gradients[3][1], gradients[4], gradients[5], gradients[6]]
    mean_list = [qkv_first, out_first, gains_first[0], gains_first[1], gate_first, up_first, down_first]
    square_list = [qkv_second, out_second, gains_second[0], gains_second[1], gate_second, up_second, down_second]
    updates = [adam_direction(weight_now, gradient, mean_old, square_old) for weight_now, gradient, mean_old, square_old in zip(weight_list, grad_list, mean_list, square_list)]
    weight_norm = jnp.sqrt(jnp.stack([jnp.sum(weight_now * weight_now) for weight_now in weight_list]))
    step_norm = jnp.sqrt(jnp.stack([jnp.sum(piece[2] * piece[2]) for piece in updates]))
    trust_ratio = weight_norm / step_norm
    masters = [weight_list[number] - LEARN_RATE * trust_ratio[number] * updates[number][2] for number in range(7)]
    clip_limit = CLIP_BASE * HD ** 0.5 / 8.0
    clip_factors = clip_limit / jnp.maximum(peak_heads, clip_limit)
    qkv_master = masters[0] * column_scale(clip_factors)[None, :]
    return (block_out.astype(jnp.bfloat16), gradients[0], qkv_master, updates[0][0], updates[0][1], masters[1], updates[1][0], updates[1][1], jnp.stack([masters[2], masters[3]]), jnp.stack([updates[2][0], updates[3][0]]), jnp.stack([updates[2][1], updates[3][1]]), masters[4], updates[4][0], updates[4][1], masters[5], updates[5][0], updates[5][1], masters[6], updates[6][0], updates[6][1], clip_factors, jnp.stack([weight_norm, step_norm]))
```

```python
import functools

import jax
import jax.numpy as jnp
from jax import lax
from jax.experimental import pallas as pl
from jax.experimental.pallas import tpu as pltpu
from jax.sharding import PartitionSpec as P

D = 1536
NH = 24
KVH = 8
HD = 64
EXPERTS = 40
TOP = 8
STEP = 10
CAP = 76
FF = 512
TP = 4
SLOTS = 80
STEP_BLOCKS = 4
FLUSH = 4
MESH = pl.DeviceIdType.MESH


RESIDUAL_SCALE = 0.22
SCORE_SCALE = 0.015625
NORM_EPS = 1e-06
ROPE_BASE = 10000.0
CLIP_BASE = 4.5
BETA_ONE = 0.9
BETA_TWO = 0.999
ADAM_EPS = 1e-06
WEIGHT_DECAY = 0.01
LEARN_RATE = 0.3
MASK_FILL = -1e30


def rope_tables(positions, head_width):
    half_width = head_width // 2
    frequency = ROPE_BASE ** (-(jnp.arange(half_width, dtype=jnp.float32) * (2.0 / head_width)))
    angles = positions.astype(jnp.float32)[:, None] * frequency[None, :]
    return (jnp.cos(angles), jnp.sin(angles))


def rotate(values, cos_table, sin_table):
    half_width = values.shape[-1] // 2
    view_shape = (cos_table.shape[0],) + (1,) * (values.ndim - 2) + (half_width,)
    cos_view = cos_table.reshape(view_shape)
    sin_view = sin_table.reshape(view_shape)
    first_half = values[..., :half_width]
    second_half = values[..., half_width:]
    return jnp.concatenate(
        [
            first_half * cos_view - second_half * sin_view,
            second_half * cos_view + first_half * sin_view,
        ],
        axis=-1,
    )


def column_scale(factor):
    per_kv = NH // KVH
    head_part = jnp.repeat(factor.reshape(KVH, per_kv), HD, axis=1)
    return jnp.concatenate([head_part, jnp.ones((KVH, 2 * HD), factor.dtype)], axis=1).reshape(-1)


def adam_direction(weight_now, gradient, mean_old, square_old):
    momentum = BETA_ONE * mean_old + (1.0 - BETA_ONE) * gradient
    variance = BETA_TWO * square_old + (1.0 - BETA_TWO) * gradient * gradient
    direction = (
        momentum / (1.0 - BETA_ONE**STEP) / (jnp.sqrt(variance / (1.0 - BETA_TWO**STEP)) + ADAM_EPS)
        + WEIGHT_DECAY * weight_now
    )
    return (momentum, variance, direction)


def norm_back(values, inverse, gain, grad_normed):
    scaled = grad_normed * gain
    average = jnp.mean(scaled * values, axis=-1, keepdims=True)
    grad_values = inverse * (scaled - values * inverse * inverse * average)
    grad_gain = jnp.sum(grad_normed * values * inverse, axis=0)
    return (grad_values, grad_gain)


def shifted(array, by):
    devices = lax.axis_size("fsdp") * lax.axis_size("seq")
    pairs = [(i, i + by) for i in range(devices) if 0 <= i + by < devices]
    return lax.ppermute(array, ("fsdp", "seq"), pairs)


class Place:
    def __init__(self, same=False):
        fsdp = lax.axis_index("fsdp")
        self.line = fsdp // 4
        self.wide = (fsdp // 2) % 2
        self.core = fsdp % 2
        self.other = lax.axis_index("seq")
        self.turned = 0 if same else self.core

    def across(self, first, second):
        wide_step = first * (1 - self.turned) + second * self.turned
        other_step = first * self.turned + second * (1 - self.turned)
        wide = self.wide + wide_step * (1 - 2 * self.wide)
        other = self.other + other_step * (1 - 2 * self.other)
        return wide, other

    def device(self, line, wide, core, other):
        return (line * 4 + wide * 2 + core, other)

    def line_at(self, turn):
        if turn == 1:
            return self.line + 1 - 2 * (self.line % 2)
        if turn == 2:
            return self.line + 2 - 4 * (self.line // 2)
        return 3 - self.line if turn == 3 else self.line

    def peer_core(self):
        return self.device(self.line, self.wide, 1 - self.core, self.other)

    def peer_first(self):
        wide, other = self.across(1, 0)
        return self.device(self.line, wide, self.core, other)

    def peer_second(self):
        wide, other = self.across(0, 1)
        return self.device(self.line, wide, self.core, other)

    def peer_line(self, side):
        return self.device(self.line + 1 - 2 * side, self.wide, self.core, self.other)

    def goes_on(self, side):
        return self.line > 0 if side else self.line < 3

    def source(self, side, distance):
        line = self.line + distance if side else self.line - distance
        return line, (line <= 3 if side else line >= 0)

    def around(self, visit, nearest=0):
        if nearest == 0:
            visit(self.line)
        for distance in (1, 2, 3):
            for side in (0, 1):
                line, valid = self.source(side, distance)

                @pl.when(valid)
                def _():
                    visit(line)

    def peer_at(self, turn):
        return self.device(self.line_at(turn), self.wide, self.core, self.other)

    def peer_turned(self, turn):
        fsdp = lax.axis_index("fsdp") + turn
        return (fsdp % 16, self.other)

    def meet(self, everyone=False, whole_line=False):
        barrier = pltpu.get_barrier_semaphore()

        def greet(peer):
            pl.semaphore_signal(barrier, inc=1, device_id=peer, device_id_type=MESH)

        if everyone:
            for turn in range(1, 16):
                greet(self.peer_turned(turn))
            greet(self.device(self.line, self.wide, self.core, 1 - self.other))
            pl.semaphore_wait(barrier, 16)
            return
        for peer in (self.peer_core(), self.peer_first(), self.peer_second()):
            greet(peer)
        if whole_line:
            for turn in (1, 2, 3):
                greet(self.peer_at(turn))
            pl.semaphore_wait(barrier, 6)
            return
        for side in (0, 1):

            @pl.when(self.goes_on(side))
            def _():
                greet(self.peer_line(side))

        ends = (self.line == 0).astype(jnp.int32) + (self.line == 3).astype(jnp.int32)
        pl.semaphore_wait(barrier, 5 - ends)


def remote(source, target, send, recv, peer):
    return pltpu.make_async_remote_copy(
        src_ref=source,
        dst_ref=target,
        send_sem=send,
        recv_sem=recv,
        device_id=peer,
        device_id_type=MESH,
    )


class Gather:
    def __init__(self, place, src_ref, out_ref, sems):
        self.place, self.src, self.out = place, src_ref, out_ref
        (
            self.keep_sem, self.core_send, self.core_recv, self.line_send, self.line_recv,
            self.first_send, self.first_recv, self.second_send, self.second_recv,
        ) = sems
        width = src_ref.shape[1] // 2
        self.half = pl.ds(pl.multiple_of(place.core * width, 128), width)

    def unit(self, line, one, two):
        wide, other = self.place.across(one, two)
        return self.out.at[line, wide, :, other, :, self.half]

    def own(self):
        place = self.place
        return self.out.at[place.line, place.wide, place.core, place.other]

    def keep(self):
        return pltpu.make_async_copy(self.src, self.own(), self.keep_sem)

    def swap(self):
        at = self.place.line
        return remote(
            self.src, self.own(), self.core_send.at[at], self.core_recv.at[at], self.place.peer_core()
        )

    def to_core(self, line, one, two):
        ref = self.unit(line, one, two)
        at = (two * 2 + one) * 4 + line
        return remote(
            ref, ref, self.core_send.at[at], self.core_recv.at[at], self.place.peer_core()
        )

    def to_first(self, line):
        ref = self.unit(line, 0, 0)
        return remote(
            ref, ref, self.first_send.at[line], self.first_recv.at[line], self.place.peer_first()
        )

    def to_second(self, line, one):
        ref = self.unit(line, one, 0)
        at = one * 4 + line
        return remote(
            ref, ref, self.second_send.at[at], self.second_recv.at[at], self.place.peer_second()
        )

    def along(self, side, line):
        ref = self.unit(line, 0, 0)
        at = side * 4 + line
        return remote(
            ref, ref, self.line_send.at[at], self.line_recv.at[at], self.place.peer_line(side)
        )

    def begin(self):
        place = self.place
        self.keep().wait()
        self.swap().wait_recv()
        self.to_second(place.line, 0).start()
        self.to_first(place.line).start()
        for side in (0, 1):

            @pl.when(place.goes_on(side))
            def _():
                self.along(side, place.line).start()

    def at_distance(self, distance, visit):
        for side in (0, 1) if distance else (0,):
            line, valid = self.place.source(side, distance)
            pl.when(valid)(functools.partial(visit, side, line))

    def arrive(self, distance):
        def visit(side, line):
            self.along(side, line).wait_recv()
            self.to_second(line, 0).start()
            self.to_first(line).start()

            @pl.when(self.place.goes_on(side))
            def _():
                self.along(side, line).start()

            self.to_core(line, 0, 0).start()

        self.at_distance(distance, visit)

    def pass_first(self, distance):
        def visit(side, line):
            self.to_first(line).wait_recv()
            self.to_second(line, 1).start()
            self.to_core(line, 1, 0).start()

        self.at_distance(distance, visit)

    def pass_second(self, one, distance):
        def visit(side, line):
            self.to_second(line, one).wait_recv()
            self.to_core(line, one, 1).start()

        self.at_distance(distance, visit)

    def finish(self):
        def end_core(line, one, two):
            copy = self.to_core(line, one, two)
            copy.wait_recv()
            copy.wait_send()

        for distance in (1, 2, 3):
            self.at_distance(distance, lambda side, line: end_core(line, 0, 0))
        self.swap().wait_send()
        for line in range(4):
            for one, two in ((1, 0), (0, 1), (1, 1)):
                end_core(line, one, two)
            self.to_first(line).wait_send()
            for one in (0, 1):
                self.to_second(line, one).wait_send()
        for side in (0, 1):

            @pl.when(self.place.goes_on(side))
            def _():
                for distance in (0, 1, 2):
                    line, valid = self.place.source(side, distance)

                    @pl.when(valid)
                    def _():
                        self.along(side, line).wait_send()


class Spread:
    def __init__(self, place, src_ref, out_ref, sems, inner):
        self.place, self.src, self.out, self.inner = place, src_ref, out_ref, inner
        self.sends, self.recvs = sems

    def copy(self, turn):
        me = lax.axis_index("fsdp")
        target = self.out.at[:, me] if self.inner else self.out.at[me]
        peer = self.place.peer_turned(turn)
        source = self.src.at[peer[0]]
        if turn == 0:
            return pltpu.make_async_copy(source, target, self.sends.at[0])
        return remote(source, target, self.sends.at[turn], self.recvs.at[turn], peer)

    def begin(self):
        for turn in (8, 7, 9, 6, 10, 5, 11, 4, 12, 3, 13, 2, 14, 1, 15, 0):
            self.copy(turn).start()

    def finish(self):
        for turn in range(16):
            self.copy(turn).wait()


GATHER_SEMS = (0, 16, 16, 8, 8, 4, 4, 8, 8)


def gather_kernel(count, moves, *refs):
    place = Place()
    if moves:
        spread = Spread(place, refs[count], refs[2 * count + 1], refs[-2:], True)
        refs = refs[:count] + refs[count + 1 : 2 * count + 1] + refs[2 * count + 2 : -2]
    sems = refs[2 * count :]
    parts = [
        Gather(
            Place(same=moves and number == count - 1),
            refs[number],
            refs[count + number],
            sems[number * len(GATHER_SEMS) : (number + 1) * len(GATHER_SEMS)],
        )
        for number in range(count)
    ]
    for part in parts:
        part.keep().start()
    place.meet(moves)
    for part in parts:
        part.swap().start()
    for part in parts:
        part.begin()
    for distance in (1, 2, 3):
        for part in parts:
            part.arrive(distance)
        if moves and distance == 2:
            spread.begin()
        for part in parts:
            part.pass_first(distance - 1)
    for part in parts:
        part.pass_first(3)
    for one in (0, 1):
        for distance in range(4):
            for part in parts:
                part.pass_second(one, distance)
    for part in parts:
        part.finish()
    if moves:
        spread.finish()


def gather_all(number, *blocks, move=None):
    dma = pltpu.SemaphoreType.DMA
    size = sum(block.shape[0] * block.shape[1] for block in blocks)
    anywhere = pl.BlockSpec(memory_space=pl.ANY)
    shapes = [jax.ShapeDtypeStruct((4, 2, 2, 2) + block.shape, block.dtype) for block in blocks]
    scratch = [dma((many,)) if many else dma for many in GATHER_SEMS] * len(blocks)
    inputs = list(blocks)
    in_specs = [pl.BlockSpec(memory_space=pltpu.VMEM)] * len(blocks)
    if move is not None:
        inputs.append(move)
        in_specs.append(anywhere)
        shape = (move.shape[1], move.shape[0]) + move.shape[2:]
        shapes.append(jax.ShapeDtypeStruct(shape, move.dtype))
        scratch += [dma((16,)), dma((16,))]
    outs = pl.pallas_call(
        functools.partial(gather_kernel, len(blocks), move is not None),
        out_shape=shapes,
        in_specs=in_specs,
        out_specs=[anywhere] * len(shapes),
        scratch_shapes=scratch,
        compiler_params=pltpu.CompilerParams(collective_id=number, has_side_effects=True),
        cost_estimate=pl.CostEstimate(flops=0, bytes_accessed=128 * size, transcendentals=0),
    )(*inputs)
    full = [out.reshape((32,) + block.shape) for out, block in zip(outs, blocks)]
    return full + list(outs[len(blocks) :])


def devices_to(fn):
    pairs = []
    for number in range(32):
        fsdp, other = divmod(number, 2)
        line, wide, core, other = fn(fsdp // 4, (fsdp // 2) % 2, fsdp % 2, other)
        pairs.append((number, (line * 4 + wide * 2 + core) * 2 + other))
    return pairs


def permuted(array, fn):
    return lax.ppermute(array, ("fsdp", "seq"), devices_to(fn))


def swap_core(array):
    return permuted(array, lambda line, wide, core, other: (line, wide, 1 - core, other))


def swap_first(array):
    return permuted(
        array, lambda line, wide, core, other: (line, wide ^ (1 - core), core, other ^ core)
    )


def swap_second(array):
    return permuted(
        array, lambda line, wide, core, other: (line, wide ^ core, core, other ^ (1 - core))
    )


def swap_line(array, turn):
    return permuted(array, lambda line, wide, core, other: (line ^ turn, wide, core, other))


def add_kernel(left_ref, right_ref, anchor_ref, out_ref):
    total = left_ref[...].astype(jnp.float32) + right_ref[...].astype(jnp.float32)
    out_ref[...] = total.astype(out_ref.dtype)


def add_after(left, right, anchor):
    block = pl.BlockSpec((1,) + left.shape[1:], lambda i: (i,) + (0,) * (left.ndim - 1))
    return pl.pallas_call(
        add_kernel,
        grid=(left.shape[0],),
        out_shape=jax.ShapeDtypeStruct(left.shape, left.dtype),
        in_specs=[block, block, pl.BlockSpec(memory_space=pl.ANY)],
        out_specs=block,
        compiler_params=pltpu.CompilerParams(vmem_limit_bytes=32 * 1024 * 1024),
    )(left, right, anchor)


class Finish:
    def __init__(self, stay, leave):
        self.stay = stay
        self.there = swap_second(leave)

    def first(self, anchor):
        stay = add_after(self.stay, self.there, anchor)
        self.stay = stay[0]
        self.there = swap_first(stay[1])

    def column(self, anchor):
        return add_after(self.stay, self.there, anchor)


def sum_kernel(beside, ending, part_ref, *refs):
    if ending:
        column_ref, out_ref, mixture_ref = refs[:3]
        chips_ref, theirs_ref, got_ref, chips_load, chips_send, chips_recv, end_sems = refs[-7:]
        refs = (out_ref,) + refs[3:-7]
    if beside:
        mix_ref, grads_ref, out_ref, *mixed_refs, moved_ref = refs[:6]
        mix_core_ref, mix_own_ref, mix_load, mix_send, mix_recv, mix_store, *spread_sems = refs[-8:]
        refs = refs[6:-8]
    else:
        out_ref, *refs = refs
    (
        own_ref, core_ref, second_ref, first_ref, line_ref, last_ref,
        load_sem, core_send, core_recv, second_send, second_recv, first_send, first_recv,
        line_send, line_recv, last_send, last_recv,
    ) = refs
    place = Place()
    rows, columns = out_ref.shape
    width = columns // 2
    half = pl.ds(pl.multiple_of(place.core * width, 128), width)
    away = pl.ds(pl.multiple_of((1 - place.core) * width, 128), width)
    piece = 16 if rows % 64 else 64
    flip = place.line // 2
    low = place.line + flip * (3 - 2 * place.line)
    lines = [line + flip * (3 - 2 * line) for line in (3, 2 - 2 * low, 1 + low, low)]

    def slot(turn, one, two):
        return turn * 4 + two * 2 + one

    def unit(turn, one, two, where):
        wide, other = place.across(one, two)
        return part_ref.at[lines[turn], wide, :, other, :, where]

    def load(turn, one, two):
        at = slot(turn, one, two)
        return pltpu.make_async_copy(unit(turn, one, two, half), own_ref.at[at], load_sem.at[at])

    def swap(turn, one, two):
        at = slot(turn, two, one)
        return remote(
            unit(turn, one, two, away),
            core_ref.at[at],
            core_send.at[at],
            core_recv.at[at],
            place.peer_core(),
        )

    def to_second(turn, one):
        at = turn * 2 + one
        return remote(
            own_ref.at[slot(turn, one, 1)],
            second_ref.at[at],
            second_send.at[at],
            second_recv.at[at],
            place.peer_second(),
        )

    def to_first(turn):
        return remote(
            own_ref.at[slot(turn, 1, 0)],
            first_ref.at[turn],
            first_send.at[turn],
            first_recv.at[turn],
            place.peer_first(),
        )

    def along(side, turn):
        at = side * 4 + lines[turn]
        return remote(
            own_ref.at[slot(turn, 0, 0)],
            line_ref.at[at],
            line_send.at[at],
            line_recv.at[at],
            place.peer_line(side),
        )

    steps = ((1, 1), (0, 1), (1, 0), (0, 0))
    for turn in range(4):
        for one, two in steps:
            load(turn, one, two).start()
    place.meet(beside, ending)
    for turn in range(4):
        for two, one in steps:
            swap(turn, one, two).start()

    def chip(turn):
        if turn == 0:
            return pltpu.make_async_copy(column_ref.at[0], chips_ref.at[0], chips_load)
        return remote(
            column_ref.at[turn],
            chips_ref.at[turn],
            chips_send.at[turn],
            chips_recv.at[turn],
            place.peer_at(turn),
        )

    def end_mixture():
        count, width_end = theirs_ref.shape
        here = pl.ds(pl.multiple_of(place.core * width_end, 128), width_end)
        there = pl.ds(pl.multiple_of((1 - place.core) * width_end, 128), width_end)
        for turn in range(4):
            chip(turn).wait()

        def body(step, carry):
            at = pl.ds(pl.multiple_of(step * 64, 64), 64)
            for kind, core in enumerate((1 - place.core, place.core)):
                total = chips_ref[0, core, at, :].astype(jnp.float32)
                for turn in (1, 2, 3):
                    total += chips_ref[turn, core, at, :].astype(jnp.float32)
                if kind:
                    mixture_ref[at, here] = total
                else:
                    theirs_ref[at, :] = total.astype(theirs_ref.dtype)
            return carry

        lax.fori_loop(0, count // 64, body, 0)
        swap_end = remote(theirs_ref, got_ref, end_sems.at[0], end_sems.at[1], place.peer_core())
        swap_end.start()
        swap_end.wait()
        mixture_ref[:, there] = got_ref[...].astype(jnp.float32)

    if ending:
        for turn in (1, 2, 3, 0):
            chip(turn).start()
    if beside:
        spread = Spread(place, grads_ref, moved_ref, spread_sems, False)

    def mix_line(at):
        return place.line_at(at % 4)

    def mix_load_copy(at):
        wide, other = place.across(at // 4 % 2, at // 8)
        return pltpu.make_async_copy(
            mix_ref.at[mix_line(at), wide, :, other, :, half],
            mix_own_ref.at[at % 2],
            mix_load.at[at % 2],
        )

    def mix_give(at):
        wide, other = place.across(at // 8, at // 4 % 2)
        return remote(
            mix_ref.at[mix_line(at), wide, :, other, :, away],
            mix_core_ref.at[at],
            mix_send.at[at],
            mix_recv.at[at],
            place.peer_core(),
        )

    def mix_store_copy(at):
        return pltpu.make_async_copy(
            mix_core_ref.at[at], mixed_refs[at // 8].at[at // 4 % 2, at % 4], mix_store.at[at]
        )

    mix_order = [8 + at for at in range(8)] + [at for at in range(8)]

    def mix_begin():
        for at in mix_order:
            mix_give(at).start()
        for at in mix_order[:2]:
            mix_load_copy(at).start()

    def mix_add(number):
        at = mix_order[number]
        mix_load_copy(at).wait()
        mix_give(at).wait_recv()
        for core in range(2):

            def body(step, carry):
                here = pl.ds(pl.multiple_of(step * piece, 16), piece)
                total = mix_own_ref[at % 2, core, here, :].astype(jnp.float32)
                total += mix_core_ref[at, core, here, :].astype(jnp.float32)
                mix_core_ref[at, core, here, :] = total.astype(mix_core_ref.dtype)
                return carry

            lax.fori_loop(0, rows // piece, body, 0)
        mix_store_copy(at).start()
        if number + 2 < 16:
            mix_load_copy(mix_order[number + 2]).start()

    def add(at, others):
        for core in range(2):

            def body(step, carry):
                here = pl.ds(pl.multiple_of(step * piece, 16), piece)
                total = own_ref[at, core, here, :].astype(jnp.float32)
                for other in others:
                    total += other[core, here, :].astype(jnp.float32)
                own_ref[at, core, here, :] = total.astype(own_ref.dtype)
                return carry

            lax.fori_loop(0, rows // piece, body, 0)

    def ready(turn, one, two):
        load(turn, one, two).wait()
        swap(turn, two, one).wait_recv()
        return core_ref.at[slot(turn, one, two)]

    def give_second(turn):
        for one in (1, 0):
            add(slot(turn, one, 1), [ready(turn, one, 1)])
            to_second(turn, one).start()

    def give_first(turn):
        others = [ready(turn, 1, 0)]
        to_second(turn, 1).wait_recv()
        add(slot(turn, 1, 0), others + [second_ref.at[turn * 2 + 1]])
        to_first(turn).start()

    def take(side, turn):
        along(side, turn).wait_recv()
        add(slot(turn, 0, 0), [line_ref.at[side * 4 + lines[turn]]])

    def give_line(turn):
        others = [ready(turn, 0, 0)]
        to_second(turn, 0).wait_recv()
        to_first(turn).wait_recv()
        add(slot(turn, 0, 0), others + [second_ref.at[turn * 2], first_ref.at[turn]])
        for side in (0, 1):
            leaves = lines[turn] < place.line if side else lines[turn] > place.line
            arrives = place.goes_on(1 - side)
            if turn == 3:
                pl.when(arrives)(functools.partial(take, side, turn))
                continue

            @pl.when(leaves)
            def _():
                pl.when(arrives)(functools.partial(take, side, turn))
                along(side, turn).start()

    plan_steps = [
        functools.partial(give_second, 0),
        functools.partial(give_second, 1),
        functools.partial(give_second, 2),
        functools.partial(give_first, 0),
        functools.partial(give_second, 3),
        functools.partial(give_first, 1),
        functools.partial(give_line, 0),
        functools.partial(give_first, 2),
        functools.partial(give_line, 1),
        functools.partial(give_first, 3),
        functools.partial(give_line, 2),
    ]
    for number, step in enumerate(plan_steps):
        step()
        if beside and number == 0:
            mix_begin()
            spread.begin()
        if beside and number >= 3:
            mix_add(2 * number - 6)
            mix_add(2 * number - 5)
    give_line(3)
    if ending:
        end_mixture()
    mine = slot(3, 0, 0)
    last = remote(
        own_ref.at[mine, 1 - place.core], last_ref, last_send, last_recv, place.peer_core()
    )
    last.start()
    out_ref[:, half] = own_ref[mine, place.core].astype(out_ref.dtype)
    last.wait_recv()
    out_ref[:, away] = last_ref[...].astype(out_ref.dtype)
    last.wait_send()
    if beside:
        for at in range(16):
            mix_give(at).wait_send()
            mix_store_copy(at).wait()
        spread.finish()
    for turn in range(4):
        for one, two in steps:
            swap(turn, one, two).wait_send()
        to_second(turn, 0).wait_send()
        to_second(turn, 1).wait_send()
        to_first(turn).wait_send()
        if turn < 3:
            for side in (0, 1):
                leaves = lines[turn] < place.line if side else lines[turn] > place.line

                @pl.when(leaves)
                def _():
                    along(side, turn).wait_send()


def sum_all(part, number, mix=None, move=None, column=None):
    rows, columns = part.shape[0] // 32, part.shape[1]
    width = columns // 2
    dma = pltpu.SemaphoreType.DMA
    kind = part.dtype
    anywhere = pl.BlockSpec(memory_space=pl.ANY)
    inputs = [part.reshape(4, 2, 2, 2, rows, columns)]
    outs = [jax.ShapeDtypeStruct((rows, columns), kind)]
    out_specs = [pl.BlockSpec(memory_space=pltpu.VMEM)]
    sems = []
    if column is not None:
        inputs.append(column)
        count, width_end = column.shape[2:]
        outs.append(jax.ShapeDtypeStruct((count, 2 * width_end), jnp.float32))
        out_specs.append(pl.BlockSpec(memory_space=pltpu.VMEM))
        sems = [
            pltpu.VMEM(column.shape, kind),
            pltpu.VMEM((count, width_end), kind),
            pltpu.VMEM((count, width_end), kind),
            dma,
            dma((4,)),
            dma((4,)),
            dma((2,)),
        ]
    if mix is not None:
        inputs.append(mix.reshape(4, 2, 2, 2, rows, columns))
        inputs.append(move)
        outs += [jax.ShapeDtypeStruct((2, 4, 2, rows, width), kind)] * 2
        outs.append(jax.ShapeDtypeStruct(move.shape, move.dtype))
        out_specs += [anywhere] * 3
        sems = [
            pltpu.VMEM((16, 2, rows, width), kind),
            pltpu.VMEM((2, 2, rows, width), kind),
            dma((2,)),
            dma((16,)),
            dma((16,)),
            dma((16,)),
            dma((16,)),
            dma((16,)),
        ]
    return pl.pallas_call(
        functools.partial(sum_kernel, mix is not None, column is not None),
        out_shape=outs,
        in_specs=[anywhere] * len(inputs),
        out_specs=out_specs,
        scratch_shapes=[
            pltpu.VMEM((16, 2, rows, width), kind),
            pltpu.VMEM((16, 2, rows, width), kind),
            pltpu.VMEM((8, 2, rows, width), kind),
            pltpu.VMEM((4, 2, rows, width), kind),
            pltpu.VMEM((8, 2, rows, width), kind),
            pltpu.VMEM((rows, width), kind),
            dma((16,)),
            dma((16,)),
            dma((16,)),
            dma((8,)),
            dma((8,)),
            dma((4,)),
            dma((4,)),
            dma((8,)),
            dma((8,)),
            dma,
            dma,
        ]
        + sems,
        compiler_params=pltpu.CompilerParams(
            collective_id=number, has_side_effects=True, vmem_limit_bytes=60 * 1024 * 1024
        ),
        cost_estimate=pl.CostEstimate(
            flops=64 * rows * columns, bytes_accessed=128 * rows * columns, transcendentals=0
        ),
    )(*inputs)


def exchange_kernel(src_ref, out_ref, sends, recvs):
    place = Place()
    place.meet()
    line, wide, core, other = place.line, place.wide, place.core, place.other
    out_ref[line, wide, core, other] = src_ref[...]

    def along(side, at_line):
        ref = out_ref.at[at_line, wide, core, other]
        at = side * 4 + at_line
        return remote(ref, ref, sends.at[at], recvs.at[at], place.peer_line(side))

    def swap(ref, at, peer):
        copy = remote(ref, ref, sends.at[at], recvs.at[at], peer)
        copy.start()
        return copy

    for side in (0, 1):

        @pl.when(place.goes_on(side))
        def _():
            along(side, line).start()

    for distance in (1, 2, 3):
        for side in (0, 1):
            from_line, valid = place.source(side, distance)

            @pl.when(valid)
            def _():
                along(side, from_line).wait_recv()

                @pl.when(place.goes_on(side))
                def _():
                    along(side, from_line).start()

    for side in (0, 1):

        @pl.when(place.goes_on(side))
        def _():
            for distance in (0, 1, 2):
                from_line, valid = place.source(side, distance)

                @pl.when(valid)
                def _():
                    along(side, from_line).wait_send()

    swap(out_ref.at[:, wide, core, other], 8, place.device(line, 1 - wide, core, other)).wait()
    swap(out_ref.at[:, :, core, other], 9, place.device(line, wide, core, 1 - other)).wait()
    swap(out_ref.at[:, :, core], 10, place.peer_core()).wait()


def exchange_all(block, number):
    out = pl.pallas_call(
        exchange_kernel,
        out_shape=jax.ShapeDtypeStruct((4, 2, 2, 2) + block.shape, block.dtype),
        in_specs=[pl.BlockSpec(memory_space=pltpu.VMEM)],
        out_specs=pl.BlockSpec(memory_space=pltpu.VMEM),
        scratch_shapes=[pltpu.SemaphoreType.DMA((11,)), pltpu.SemaphoreType.DMA((11,))],
        compiler_params=pltpu.CompilerParams(collective_id=number, has_side_effects=True),
    )(block)
    return out.reshape((32,) + block.shape)


class Plan:
    def __init__(self):
        self.fsdp = lax.axis_size("fsdp")
        self.seq = lax.axis_size("seq")
        self.exp_dev = EXPERTS // self.seq
        self.units = self.exp_dev // (TP + 1)
        self.copies = self.fsdp // (TP * self.units)
        members = TP * self.units
        self.members = members
        self.near = [[c * members + i for i in range(members)] for c in range(self.copies)]
        self.far = [[c * members + i for c in range(self.copies)] for i in range(members)]
        self.blocks = members * self.seq
        self.plain = self.copies == 1
        self.direct = self.fsdp == 16 and self.seq == 2


def gather_attention(plan, qkv_weight, out_weight, norm_gains, routing, cots, packed):
    qkv_weight = qkv_weight.astype(jnp.bfloat16)
    out_weight = out_weight.astype(jnp.bfloat16)
    norm_gains = norm_gains.astype(jnp.bfloat16)
    if not plan.direct:
        return (
            lax.all_gather(qkv_weight, ("fsdp", "seq"), axis=0, tiled=True),
            lax.all_gather(out_weight, ("fsdp", "seq"), axis=0, tiled=True),
            lax.all_gather(norm_gains, ("fsdp", "seq"), axis=1, tiled=True),
            gather_tokens(plan, routing),
            gather_tokens(plan, cots).reshape(-1, D),
            send_weights(plan, packed),
        )
    rows, extra = qkv_weight.shape[0], routing.shape[1]
    wide_gains = jnp.pad(norm_gains, ((0, rows - 2 - routing.shape[0]), (0, extra - rows)))
    block = jnp.concatenate(
        [out_weight, jnp.concatenate([routing, wide_gains], axis=0)], axis=1
    )
    qkv_full, full, all_cots, weights = gather_all(0, qkv_weight, block, cots, move=packed)
    ends = out_weight.shape[1]
    at = routing.shape[0]
    return (
        qkv_full.reshape(D, -1),
        full[:, :, :ends].reshape(D, ends),
        jnp.transpose(full[:, at : at + 2, ends : ends + rows], (1, 0, 2)).reshape(2, D),
        full[:, :at, ends:],
        all_cots.reshape(-1, D),
        weights.reshape(3, D, weights.shape[3]),
    )


def sum_attention(plan, qkv_grad, out_grad, gains_grad, column):
    if not plan.direct:
        return (
            lax.psum_scatter(qkv_grad, ("fsdp", "seq"), scatter_dimension=0, tiled=True),
            lax.psum_scatter(out_grad, ("fsdp", "seq"), scatter_dimension=0, tiled=True),
            lax.psum_scatter(gains_grad, ("fsdp", "seq"), scatter_dimension=1, tiled=True),
            column,
        )
    split = qkv_grad.shape[1]
    ends = split + out_grad.shape[1]
    gains = jnp.pad(jnp.transpose(gains_grad), ((0, 0), (0, 254)))
    block = jnp.concatenate(
        [piece.astype(jnp.bfloat16) for piece in (qkv_grad, out_grad, gains)], axis=1
    )
    total, mixture = sum_all(block, 3, column=column)
    total = total.astype(jnp.float32)
    gains = jnp.transpose(total[:, ends : ends + 2])
    return total[:, :split], total[:, split:ends], gains, mixture


def gather_rows(plan, rows):
    if not plan.direct:
        return gather_tokens(plan, rows).reshape(-1, D)
    return gather_all(1, rows)[0].reshape(-1, D)


class Whole:
    def __init__(self, plan, part):
        self.total = scatter_tokens(plan, part)

    def first(self, anchor):
        pass

    def column(self, anchor):
        return self.total


def sum_rows(plan, back, mix, gate_grads, grads):
    gate_grads = return_grads(plan, gate_grads)
    if not plan.direct:
        return scatter_tokens(plan, back), Whole(plan, mix), gate_grads, return_grads(plan, grads)
    back, stay, leave, grads = sum_all(back, 2, mix=mix, move=grads)
    return back, Finish(stay, leave), gate_grads, grads


def share_stats(plan, stats):
    if not plan.direct:
        return lax.all_gather(stats, ("fsdp", "seq"), axis=0)
    block = jnp.pad(stats[None, :], ((0, 7), (0, 128 - stats.shape[0])))
    return exchange_all(block, 4)[:, 0, : stats.shape[0]]


def gather_tokens(plan, block):
    if plan.plain:
        return lax.all_gather(block, ("fsdp", "seq"), axis=0)
    block = lax.all_gather(block, "seq", axis=0)
    block = lax.all_gather(block, "fsdp", axis=0, axis_index_groups=plan.near)
    return block.reshape((plan.blocks,) + block.shape[2:])


def scatter_tokens(plan, partial):
    if plan.plain:
        return lax.psum_scatter(partial, ("fsdp", "seq"), scatter_dimension=0, tiled=True)
    partial = lax.psum_scatter(
        partial, "fsdp", scatter_dimension=0, tiled=True, axis_index_groups=plan.near
    )
    return lax.psum_scatter(partial, "seq", scatter_dimension=0, tiled=True)


def pack_kernel(gate_ref, up_ref, down_ref, out_ref):
    part = FF // TP
    for tensor, ref in enumerate((gate_ref, up_ref, down_ref)):
        for member in range(TP):
            out_ref[member, tensor, :, :FF] = ref[member].astype(jnp.bfloat16)
            out_ref[member, tensor, :, FF:] = ref[TP, :, member * part : (member + 1) * part].astype(
                jnp.bfloat16
            )


def pack_experts(plan, gate_weight, up_weight, down_weight):
    rows = gate_weight.shape[1]
    width = FF + FF // TP
    block = pl.BlockSpec((TP + 1, rows, FF), lambda i: (i, 0, 0))
    return pl.pallas_call(
        pack_kernel,
        grid=(plan.units,),
        out_shape=jax.ShapeDtypeStruct((plan.members, 3, rows, width), jnp.bfloat16),
        in_specs=[block] * 3,
        out_specs=pl.BlockSpec((TP, 3, rows, width), lambda i: (i, 0, 0, 0)),
        compiler_params=pltpu.CompilerParams(vmem_limit_bytes=32 * 1024 * 1024),
    )(gate_weight, up_weight, down_weight)


def lamb_kernel(*refs):
    weight_refs, first_refs, second_refs = refs[0:3], refs[3:6], refs[6:9]
    gates_ref, grads_ref = refs[9], refs[10]
    momentum_refs, variance_refs, direction_refs, sums_ref = refs[12:15], refs[15:18], refs[18:21], refs[21]
    part = FF // TP

    @pl.when(pl.program_id(0) == 0)
    def _():
        sums_ref[...] = jnp.zeros_like(sums_ref)

    for tensor in range(3):
        squares = [0.0, 0.0]
        for expert in range(TP + 1):
            def grad_of(member, columns):
                if tensor:
                    return grads_ref[member, tensor - 1, :, columns]
                return gates_ref[member, :, columns]

            if expert < TP:
                grad = grad_of(expert, slice(0, FF))
            else:
                grad = jnp.concatenate(
                    [grad_of(member, slice(FF, FF + part)) for member in range(TP)], axis=1
                )
            weight = weight_refs[tensor][expert]
            momentum, variance, direction = adam_direction(
                weight,
                grad.astype(jnp.float32),
                first_refs[tensor][expert],
                second_refs[tensor][expert],
            )
            momentum_refs[tensor][expert] = momentum
            variance_refs[tensor][expert] = variance
            direction_refs[tensor][expert] = direction
            squares[0] += weight * weight
            squares[1] += direction * direction
        for kind in range(2):
            rows = squares[kind].reshape(-1, 8, FF)
            total = jnp.sum(rows, axis=0)
            for lane in range(0, FF, 128):
                sums_ref[2 * tensor + kind] += total[:, lane : lane + 128]


def lamb_experts(plan, weights, firsts, seconds, gates, packed, anchor):
    rows = weights[0].shape[1]
    shape = jax.ShapeDtypeStruct(weights[0].shape, jnp.float32)
    block = pl.BlockSpec((TP + 1, rows, FF), lambda i: (i, 0, 0))
    outs = pl.pallas_call(
        lamb_kernel,
        grid=(plan.units,),
        out_shape=[shape] * 9 + [jax.ShapeDtypeStruct((8, 8, 128), jnp.float32)],
        in_specs=[block] * 9
        + [
            pl.BlockSpec((TP, rows, packed.shape[3]), lambda i: (i, 0, 0)),
            pl.BlockSpec((TP, 2, rows, packed.shape[3]), lambda i: (i, 0, 0, 0)),
            pl.BlockSpec(memory_space=pl.ANY),
        ],
        out_specs=[block] * 9 + [pl.BlockSpec((8, 8, 128), lambda i: (0, 0, 0))],
        compiler_params=pltpu.CompilerParams(vmem_limit_bytes=56 * 1024 * 1024),
        cost_estimate=pl.CostEstimate(
            flops=60 * weights[0].size,
            bytes_accessed=80 * weights[0].size,
            transcendentals=6 * weights[0].size,
        ),
    )(*weights, *firsts, *seconds, gates, packed, anchor)
    sums = jnp.sum(outs[9], axis=(1, 2))
    return list(zip(outs[0:3], outs[3:6], outs[6:9])), sums[0:6:2], sums[1:6:2]


def send_weights(plan, packed):
    if plan.copies == 1:
        got = lax.all_to_all(packed, "fsdp", split_axis=0, concat_axis=0, tiled=True)
    else:
        got = lax.all_to_all(
            packed, "fsdp", split_axis=0, concat_axis=0, tiled=True, axis_index_groups=plan.near
        )
        got = lax.all_gather(got, "fsdp", axis=0, tiled=True, axis_index_groups=plan.far)
    return jnp.transpose(got, (1, 0, 2, 3)).reshape(3, D, got.shape[3])


def return_grads(plan, blocks):
    if plan.copies > 1:
        blocks = lax.psum_scatter(
            blocks, "fsdp", scatter_dimension=0, tiled=True, axis_index_groups=plan.far
        )
        return lax.all_to_all(
            blocks, "fsdp", split_axis=0, concat_axis=0, tiled=True, axis_index_groups=plan.near
        )
    return lax.all_to_all(blocks, "fsdp", split_axis=0, concat_axis=0, tiled=True)


def route_table(plan, packed, experts):
    routed = packed[:, :TOP]
    gates = packed[:, TOP:].astype(jnp.float32)
    tokens = packed.shape[-1]
    earlier = (
        jnp.arange(tokens, dtype=jnp.int32)[:, None] <= jnp.arange(tokens, dtype=jnp.int32)[None, :]
    ).astype(jnp.bfloat16)
    ranks = []
    weights = []
    for expert in experts:
        match = routed == expert.astype(jnp.bfloat16)
        here = jnp.any(match, axis=1)
        order = jnp.dot(
            here.astype(jnp.bfloat16), earlier, preferred_element_type=jnp.float32
        )
        ranks.append(jnp.where(here, order - 1.0, -1.0))
        weights.append(jnp.sum(jnp.where(match, gates, 0.0), axis=1))
    filler = jnp.zeros_like(ranks[0])
    return jnp.stack(ranks + weights + [filler] * 4, axis=1)


NATURAL = (((1,), (0,)), ((), ()))
RIGHT_TURNED = (((1,), (1,)), ((), ()))
LEFT_TURNED = (((0,), (0,)), ((), ()))


def product(left, right, dims=NATURAL):
    return lax.dot_general(left, right, dims, preferred_element_type=jnp.float32)


def expert_kernel(
    steps, tokens, table_ref, rows_ref, cots_ref, weights_ref, out_ref, back_ref, gates_ref,
    grads_ref, total_ref, picked_ref, pulled_ref, result_ref, return_ref,
):
    step = pl.program_id(0)
    grad_rows = grads_ref.shape[2]

    @pl.when(step == 0)
    def _():
        total_ref[...] = jnp.zeros_like(total_ref)

    @pl.when(step < steps)
    def _():
        slot_of = lax.broadcasted_iota(jnp.int32, (SLOTS, tokens), 0).astype(jnp.float32)

        def spread_table(block, first):
            chosen = [slot_of == table_ref[block, unit : unit + 1, :] for unit in range(2)]
            if first is None:
                return jnp.concatenate([jnp.where(one, 1.0, 0.0) for one in chosen], axis=0)
            return jnp.concatenate(
                [
                    jnp.where(one, table_ref[block, first + unit : first + unit + 1, :], 0.0)
                    for unit, one in enumerate(chosen)
                ],
                axis=0,
            )

        for block in range(STEP_BLOCKS):
            hot = spread_table(block, None).astype(jnp.bfloat16)
            gate = jnp.sum(spread_table(block, 2), axis=1, keepdims=True)
            own = pl.ds(block * tokens, tokens)
            place = pl.ds(block * SLOTS, SLOTS)
            picked = product(hot, rows_ref[own, :]).astype(jnp.bfloat16)
            pulled = (RESIDUAL_SCALE * gate * product(hot, cots_ref[own, :])).astype(jnp.bfloat16)
            for unit in range(2):
                half = slice(unit * SLOTS, (unit + 1) * SLOTS)
                picked_ref[unit, place, :] = picked[half]
                pulled_ref[unit, place, :] = pulled[half]
        for unit, columns in ((0, pl.ds(0, FF)), (1, pl.ds(FF, FF // TP))):
            rows = picked_ref[unit]
            cots = pulled_ref[unit]
            gate_weight = weights_ref[0, :, columns]
            up_weight = weights_ref[1, :, columns]
            down_weight = weights_ref[2, :, columns]
            gate_pre = product(rows, gate_weight)
            up_pre = product(rows, up_weight)
            grad_act = product(cots, down_weight)
            sigmoid_gate = jax.nn.sigmoid(gate_pre)
            activated = gate_pre * sigmoid_gate
            hidden_act = (activated * up_pre).astype(jnp.bfloat16)
            slope = sigmoid_gate * (1.0 + gate_pre * (1.0 - sigmoid_gate))
            grad_gate = (grad_act * up_pre * slope).astype(jnp.bfloat16)
            grad_up = (grad_act * activated).astype(jnp.bfloat16)
            result_ref[unit] = product(hidden_act, down_weight, RIGHT_TURNED).astype(jnp.bfloat16)
            return_ref[unit] = (
                product(grad_gate, gate_weight, RIGHT_TURNED)
                + product(grad_up, up_weight, RIGHT_TURNED)
            ).astype(jnp.bfloat16)
            total_ref[0, :, columns] += product(rows, grad_gate, LEFT_TURNED)
            total_ref[1, :, columns] += product(rows, grad_up, LEFT_TURNED)
            total_ref[2, :, columns] += product(cots, hidden_act, LEFT_TURNED)
        for block in range(STEP_BLOCKS):
            own = pl.ds(block * tokens, tokens)
            place = pl.ds(block * SLOTS, SLOTS)

            def both(ref):
                return jnp.concatenate([ref[0, place, :], ref[1, place, :]], axis=0)

            hot = spread_table(block, None).astype(jnp.bfloat16)
            gated = spread_table(block, 2).astype(jnp.bfloat16)
            out_ref[own, :] = product(gated, both(result_ref), LEFT_TURNED).astype(jnp.bfloat16)
            back_ref[own, :] = product(hot, both(return_ref), LEFT_TURNED).astype(jnp.bfloat16)

    @pl.when(step >= steps)
    def _():
        per_step = grads_ref.shape[0]
        for piece in range(per_step):
            first = pl.multiple_of(((step - steps) * per_step + piece) * grad_rows, 16)
            for tensor in range(3):
                grad = total_ref[tensor, pl.ds(first, grad_rows), :].astype(jnp.bfloat16)
                if tensor:
                    grads_ref[piece, tensor - 1] = grad
                else:
                    gates_ref[piece] = grad


def run_experts(table, rows, cots, weights, owners):
    blocks, _, tokens = table.shape
    steps = blocks // STEP_BLOCKS
    width = weights.shape[2]
    grad_rows = D // owners
    last = steps - 1
    chunk = STEP_BLOCKS * tokens
    stream = pl.BlockSpec((chunk, D), lambda i: (jnp.minimum(i, last), 0))
    slots = STEP_BLOCKS * SLOTS
    return pl.pallas_call(
        functools.partial(expert_kernel, steps, tokens),
        grid=(steps + FLUSH,),
        out_shape=(
            jax.ShapeDtypeStruct((blocks * tokens, D), jnp.bfloat16),
            jax.ShapeDtypeStruct((blocks * tokens, D), jnp.bfloat16),
            jax.ShapeDtypeStruct((owners, grad_rows, width), jnp.bfloat16),
            jax.ShapeDtypeStruct((owners, 2, grad_rows, width), jnp.bfloat16),
        ),
        in_specs=[
            pl.BlockSpec((STEP_BLOCKS, 8, tokens), lambda i: (jnp.minimum(i, last), 0, 0)),
            stream,
            stream,
            pl.BlockSpec((3, D, width), lambda i: (0, 0, 0), pipeline_mode=pl.Buffered(1)),
        ],
        out_specs=(
            stream,
            stream,
            pl.BlockSpec(
                (owners // FLUSH, grad_rows, width), lambda i: (jnp.maximum(i - steps, 0), 0, 0)
            ),
            pl.BlockSpec(
                (owners // FLUSH, 2, grad_rows, width),
                lambda i: (jnp.maximum(i - steps, 0), 0, 0, 0),
            ),
        ),
        scratch_shapes=[
            pltpu.VMEM((3, D, width), jnp.float32),
            pltpu.VMEM((2, slots, D), jnp.bfloat16),
            pltpu.VMEM((2, slots, D), jnp.bfloat16),
            pltpu.VMEM((2, slots, D), jnp.bfloat16),
            pltpu.VMEM((2, slots, D), jnp.bfloat16),
        ],
        compiler_params=pltpu.CompilerParams(vmem_limit_bytes=62 * 1024 * 1024),
        cost_estimate=pl.CostEstimate(
            flops=blocks * SLOTS * 2 * D * (9 * width + 8 * tokens),
            bytes_accessed=blocks * tokens * D * 8 + 3 * D * width * 4,
            transcendentals=blocks * SLOTS * width,
        ),
    )(table, rows, cots, weights)


def local(
    hidden_in,
    grad_out,
    routes,
    gate_weights,
    doc_start,
    qkv_weight,
    qkv_first,
    qkv_second,
    out_weight,
    out_first,
    out_second,
    norm_gains,
    gains_first,
    gains_second,
    gate_weight,
    gate_first,
    gate_second,
    up_weight,
    up_first,
    up_second,
    down_weight,
    down_first,
    down_second,
):
    plan = Plan()
    seq_index = lax.axis_index("seq")
    fsdp_index = lax.axis_index("fsdp")
    seq_count = plan.seq
    tok_rows = hidden_in.shape[0]
    per_kv = NH // KVH
    group_width = (per_kv + 2) * HD
    out_weight, out_first, out_second = (jnp.transpose(a) for a in (out_weight, out_first, out_second))
    down_weight, down_first, down_second = (
        jnp.transpose(a, (0, 2, 1)) for a in (down_weight, down_first, down_second)
    )

    qkv_full, out_full, gains_full, all_routes, all_cots, expert_weights = gather_attention(
        plan,
        qkv_weight,
        out_weight,
        norm_gains,
        jnp.concatenate([jnp.transpose(routes).astype(jnp.bfloat16), jnp.transpose(gate_weights)]),
        grad_out,
        pack_experts(plan, gate_weight, up_weight, down_weight),
    )
    member = lax.rem(fsdp_index, plan.members)
    first_expert = seq_index * plan.exp_dev + (member // TP) * (TP + 1)
    table = route_table(plan, all_routes, (first_expert + lax.rem(member, TP), first_expert + TP))

    attn_gain = gains_full[0].astype(jnp.float32)
    ffn_gain = gains_full[1].astype(jnp.float32)
    hidden = hidden_in.astype(jnp.float32)
    inverse_one = lax.rsqrt(jnp.mean(hidden * hidden, axis=-1, keepdims=True) + NORM_EPS)
    normed_one = (hidden * inverse_one * attn_gain).astype(jnp.bfloat16)
    projected = jnp.dot(normed_one, qkv_full, preferred_element_type=jnp.float32).reshape(
        tok_rows, KVH, group_width
    )
    first_token = (fsdp_index * seq_count + seq_index) * tok_rows
    token_pos = first_token + jnp.arange(tok_rows, dtype=jnp.int32)
    own_starts = lax.dynamic_slice_in_dim(doc_start, seq_index * tok_rows, tok_rows)
    cos_table, sin_table = rope_tables(token_pos - own_starts, HD)
    turned = rotate(
        projected[:, :, : (per_kv + 1) * HD].reshape(tok_rows, KVH, per_kv + 1, HD),
        cos_table,
        sin_table,
    ).astype(jnp.bfloat16)
    queries = turned[:, :, :per_kv]
    keyvals = jnp.concatenate(
        [turned[:, :, per_kv], projected[:, :, (per_kv + 1) * HD :].astype(jnp.bfloat16)], axis=-1
    )
    both_kv = jnp.concatenate(
        [shifted(keyvals, by) for by in range(seq_count, 0, -1)] + [keyvals], axis=0
    )
    keys_all = both_kv[:, :, :HD]
    values_all = both_kv[:, :, HD:]
    key_count = (seq_count + 1) * tok_rows
    key_pos = first_token - seq_count * tok_rows + jnp.arange(key_count, dtype=jnp.int32)
    allowed = (key_pos[None, :] >= own_starts[:, None]) & (key_pos[None, :] <= token_pos[:, None])
    scores = (
        jnp.einsum("qjid,kjd->jiqk", queries, keys_all, preferred_element_type=jnp.float32)
        * SCORE_SCALE
    )
    masked = jnp.where(allowed, scores, MASK_FILL)
    row_peak = jnp.max(masked, axis=-1, keepdims=True)
    exponent = jnp.where(allowed, jnp.exp(masked - row_peak), 0.0)
    row_total = jnp.sum(exponent, axis=-1, keepdims=True)
    attn_probs = exponent / row_total
    rounded = attn_probs.astype(jnp.bfloat16)
    attn_tokens = (
        jnp.einsum("jiqk,kjd->qjid", rounded, values_all, preferred_element_type=jnp.float32)
        .astype(jnp.bfloat16)
        .reshape(tok_rows, NH * HD)
    )
    head_peak = jnp.max(row_peak, axis=(2, 3)).reshape(NH)

    after_attn = hidden + RESIDUAL_SCALE * lax.dot_general(
        attn_tokens, out_full, RIGHT_TURNED, preferred_element_type=jnp.float32
    )
    inverse_two = lax.rsqrt(jnp.mean(after_attn * after_attn, axis=-1, keepdims=True) + NORM_EPS)
    normed_two = (after_attn * inverse_two * ffn_gain).astype(jnp.bfloat16)
    all_rows = gather_rows(plan, normed_two)
    mix_part, back_part, gate_grads, expert_grads = run_experts(
        table, all_rows, all_cots, expert_weights, plan.fsdp
    )
    back_sum, mix_sum, own_gates, own_grads = sum_rows(
        plan, back_part, mix_part, gate_grads, expert_grads
    )
    grad_normed_two = back_sum.astype(jnp.float32)
    back_two, gain_grad_two = norm_back(after_attn, inverse_two, ffn_gain, grad_normed_two)
    grad_after = grad_out.astype(jnp.float32) + back_two
    grad_attn = (RESIDUAL_SCALE * grad_after).astype(jnp.bfloat16)
    out_grad = jnp.einsum("tc,td->dc", attn_tokens, grad_attn, preferred_element_type=jnp.float32)
    grad_mixed = (
        jnp.dot(grad_attn, out_full, preferred_element_type=jnp.float32)
        .astype(jnp.bfloat16)
        .reshape(tok_rows, KVH, per_kv, HD)
    )
    grad_probs = jnp.einsum(
        "qjid,kjd->jiqk", grad_mixed, values_all, preferred_element_type=jnp.float32
    )
    centre = jnp.sum(attn_probs * grad_probs, axis=-1, keepdims=True)
    grad_scores = (attn_probs * (grad_probs - centre)).astype(jnp.bfloat16)
    grad_query = (
        jnp.einsum("jiqk,kjd->qjid", grad_scores, keys_all, preferred_element_type=jnp.float32)
        * SCORE_SCALE
    )
    grad_key = (
        jnp.einsum("jiqk,qjid->kjd", grad_scores, queries, preferred_element_type=jnp.float32)
        * SCORE_SCALE
    )
    grad_value = jnp.einsum(
        "jiqk,qjid->kjd", rounded, grad_mixed, preferred_element_type=jnp.float32
    )
    grad_kv = jnp.concatenate([grad_key, grad_value], axis=-1)
    mix_sum.first(grad_query[:8, 0, 0])
    own_kv = grad_kv[seq_count * tok_rows :]
    for by in range(seq_count, 0, -1):
        piece = grad_kv[(seq_count - by) * tok_rows : (seq_count - by + 1) * tok_rows]
        own_kv = own_kv + shifted(piece.astype(jnp.bfloat16), -by).astype(jnp.float32)
    query_key = jnp.concatenate([grad_query, own_kv[:, :, None, :HD]], axis=2)
    unturned = rotate(query_key, cos_table, -sin_table).reshape(tok_rows, KVH, (per_kv + 1) * HD)
    grad_projected = (
        jnp.concatenate([unturned, own_kv[:, :, HD:]], axis=2)
        .astype(jnp.bfloat16)
        .reshape(tok_rows, KVH * group_width)
    )
    qkv_grad = jnp.einsum(
        "tc,tq->cq", normed_one, grad_projected, preferred_element_type=jnp.float32
    )
    grad_normed_one = jnp.einsum(
        "tq,cq->tc", grad_projected, qkv_full, preferred_element_type=jnp.float32
    )
    back_one, gain_grad_one = norm_back(hidden, inverse_one, attn_gain, grad_normed_one)
    input_grad = grad_after + back_one
    gains_grad = jnp.stack([gain_grad_one, gain_grad_two])
    summed_qkv, summed_out, summed_gains, mixture = sum_attention(
        plan, qkv_grad, out_grad, gains_grad, mix_sum.column(grad_projected[:8, :128])
    )
    block_output = (after_attn + RESIDUAL_SCALE * mixture.astype(jnp.float32)).astype(jnp.bfloat16)
    weight_list = [
        qkv_weight,
        out_weight,
        norm_gains[0],
        norm_gains[1],
        gate_weight,
        up_weight,
        down_weight,
    ]
    grad_list = [summed_qkv, summed_out, summed_gains[0], summed_gains[1]]
    mean_list = [qkv_first, out_first, gains_first[0], gains_first[1]]
    square_list = [qkv_second, out_second, gains_second[0], gains_second[1]]
    updates = [
        adam_direction(weight_now, gradient, mean_old, square_old)
        for weight_now, gradient, mean_old, square_old in zip(
            weight_list[:4], grad_list, mean_list, square_list
        )
    ]
    expert_updates, expert_weight, expert_step = lamb_experts(
        plan,
        weight_list[4:],
        [gate_first, up_first, down_first],
        [gate_second, up_second, down_second],
        own_gates,
        own_grads,
        grad_query[:8, 0, 0],
    )
    local_weight = jnp.concatenate(
        [
            jnp.stack([jnp.sum(weight_now * weight_now) for weight_now in weight_list[:4]]),
            expert_weight,
        ]
    )
    local_step = jnp.concatenate(
        [jnp.stack([jnp.sum(piece[2] * piece[2]) for piece in updates]), expert_step]
    )
    updates += expert_updates
    stats = share_stats(plan, jnp.concatenate([local_weight, local_step, head_peak]))
    weight_norm = jnp.sqrt(jnp.sum(stats[:, :7], axis=0))
    step_norm = jnp.sqrt(jnp.sum(stats[:, 7:14], axis=0))
    peak_heads = jnp.max(stats[:, 14:], axis=0)
    trust_ratio = weight_norm / step_norm
    masters = [
        weight_list[number] - LEARN_RATE * trust_ratio[number] * updates[number][2]
        for number in range(7)
    ]
    clip_limit = CLIP_BASE * HD**0.5 / 8.0
    clip_factors = clip_limit / jnp.maximum(peak_heads, clip_limit)
    qkv_master = masters[0] * column_scale(clip_factors)[None, :]
    return (
        block_output,
        input_grad,
        qkv_master,
        updates[0][0],
        updates[0][1],
        jnp.transpose(masters[1]),
        jnp.transpose(updates[1][0]),
        jnp.transpose(updates[1][1]),
        jnp.stack([masters[2], masters[3]]),
        jnp.stack([updates[2][0], updates[3][0]]),
        jnp.stack([updates[2][1], updates[3][1]]),
        masters[4],
        updates[4][0],
        updates[4][1],
        masters[5],
        updates[5][0],
        updates[5][1],
        jnp.transpose(masters[6], (0, 2, 1)),
        jnp.transpose(updates[6][0], (0, 2, 1)),
        jnp.transpose(updates[6][1], (0, 2, 1)),
        clip_factors,
        jnp.stack([weight_norm, step_norm]),
    )


def solution(mesh):
    return jax.shard_map(
        local,
        mesh=mesh,
        in_specs=(
            P(("fsdp", "seq"), None),
            P(("fsdp", "seq"), None),
            P(("fsdp", "seq"), None),
            P(("fsdp", "seq"), None),
            P("fsdp"),
            P(("fsdp", "seq"), None),
            P(("fsdp", "seq"), None),
            P(("fsdp", "seq"), None),
            P(None, ("fsdp", "seq")),
            P(None, ("fsdp", "seq")),
            P(None, ("fsdp", "seq")),
            P(None, ("fsdp", "seq")),
            P(None, ("fsdp", "seq")),
            P(None, ("fsdp", "seq")),
            P("seq", "fsdp", None),
            P("seq", "fsdp", None),
            P("seq", "fsdp", None),
            P("seq", "fsdp", None),
            P("seq", "fsdp", None),
            P("seq", "fsdp", None),
            P("seq", None, "fsdp"),
            P("seq", None, "fsdp"),
            P("seq", None, "fsdp"),
        ),
        out_specs=(
            P(("fsdp", "seq"), None),
            P(("fsdp", "seq"), None),
            P(("fsdp", "seq"), None),
            P(("fsdp", "seq"), None),
            P(("fsdp", "seq"), None),
            P(None, ("fsdp", "seq")),
            P(None, ("fsdp", "seq")),
            P(None, ("fsdp", "seq")),
            P(None, ("fsdp", "seq")),
            P(None, ("fsdp", "seq")),
            P(None, ("fsdp", "seq")),
            P("seq", "fsdp", None),
            P("seq", "fsdp", None),
            P("seq", "fsdp", None),
            P("seq", "fsdp", None),
            P("seq", "fsdp", None),
            P("seq", "fsdp", None),
            P("seq", None, "fsdp"),
            P("seq", None, "fsdp"),
            P("seq", None, "fsdp"),
            P(),
            P(),
        ),
        check_vma=False,
    )
```
